256 devices in a mesh: pair: 32 (over z, y), row: 8 (over x, core).
Axes of the slice: x: 4, y: 4, z: 8, core: 2. Of those that a mesh axis runs over, the one named last changes fastest.
Arguments:
- matrix: float32 [32768, 8192], P('row', 'pair'), may hold values from -54 to 54
Outputs:
- magnitudes: float32 [32768, 8192], P('row', 'pair')
- energies: float32 [8192], P('pair')
The draws below stay inside these ranges and needn't reach their ends.
All inputs are finite; a program needn't handle non-finite values.
Results may differ from the reference program's by a relative error of at most 0.0003.
Values sent between devices are 32-bit elements; how exact they have to be, the bound alone decides.
No kernel may reach another device: no remote copies, remote signals or barrier semaphores. Data moves between devices by JAX's collectives and lax.ppermute only.
A program may use at most 64 MiB of HBM per device.

```python
import math
import jax
import jax.numpy as jnp
import numpy as np
from jax import lax

BLOCK = 128
STEPS = 16
ROWS = 32768
COLS = 8192
N_PAIR = 32


def draw_matrix(key, part):
    key = jax.random.fold_in(key, 7)
    subkeys = jax.random.split(key, 3)
    row_scale = jnp.exp(jax.random.uniform(subkeys[0], (ROWS, 1), jnp.float32, math.log(0.3), math.log(3.0)))
    col_scale = jnp.exp(jax.random.uniform(subkeys[1], (1, COLS), jnp.float32, math.log(0.3), math.log(3.0)))
    basic_part = jnp.clip(jax.random.normal(subkeys[2], (ROWS, COLS), jnp.float32), -6.0, 6.0)
    return basic_part * row_scale * col_scale


def setup_inputs(seed: int = 0) -> dict:
    streams_of = jax.random.split(jax.random.key(seed), 2)
    return {
        "matrix": draw_matrix(jax.random.fold_in(streams_of[1], 71), 0),
    }


precise = lax.Precision.HIGHEST


def rotate_pairs(entries, cos_part, sin_part, which_axis):
    middle = entries.shape[which_axis] // 2
    if which_axis == 1:
        leading = entries[:, :middle]
        trailing = entries[:, middle:]
        cos_row = cos_part[None, :]
        sin_row = sin_part[None, :]
        return jnp.concatenate([cos_row * leading - sin_row * trailing, sin_row * leading + cos_row * trailing], axis=1)
    leading = entries[:middle]
    trailing = entries[middle:]
    cos_col = cos_part[:, None]
    sin_col = sin_part[:, None]
    return jnp.concatenate([cos_col * leading - sin_col * trailing, sin_col * leading + cos_col * trailing], axis=0)


def reorder(entries, which_axis):
    middle = entries.shape[which_axis] // 2
    bounds = [(0, 1), (middle, middle + 1), (1, middle - 1), (middle + 1, 2 * middle), (middle - 1, middle)]
    return jnp.concatenate([lax.slice_in_dim(entries, first_at, last_at, axis=which_axis) for first_at, last_at in bounds], axis=which_axis)


def restore_table(order_size, step_count):
    labels = np.arange(order_size)
    middle = order_size // 2
    for number in range(step_count):
        labels = np.concatenate([labels[0:1], labels[middle:middle + 1], labels[1:middle - 1], labels[middle + 1:], labels[middle - 1:middle]])
    restore = np.argsort(labels)
    return np.eye(order_size, dtype=np.float32)[:, restore]


def jacobi_step(step_index, carried):
    products, rotation = carried
    middle = products.shape[0] // 2
    diagonal = jnp.diagonal(products)
    coupling = jnp.diagonal(products, offset=middle)
    angles = 0.5 * jnp.arctan2(-2.0 * coupling, diagonal[:middle] - diagonal[middle:])
    cos_part = jnp.cos(angles)
    sin_part = jnp.sin(angles)
    products = rotate_pairs(rotate_pairs(products, cos_part, sin_part, 1), cos_part, sin_part, 0)
    rotation = rotate_pairs(rotation, cos_part, sin_part, 1)
    return reorder(reorder(products, 0), 1), reorder(rotation, 1)


def eigensolve(products):
    rotation = jnp.eye(products.shape[0], dtype=jnp.float32)
    products, rotation = lax.fori_loop(0, STEPS, jacobi_step, (products, rotation))
    table = jnp.asarray(restore_table(products.shape[0], STEPS), dtype=jnp.float32)
    return jnp.dot(rotation, table, precision=precise, preferred_element_type=jnp.float32)


def panel_product(left_panel, right_panel):
    return jnp.einsum("ri,rj->ij", left_panel, right_panel, precision=precise, preferred_element_type=jnp.float32)


def reference(matrix):
    pair_width = 2 * BLOCK
    grouped = matrix.reshape(ROWS, N_PAIR, pair_width)
    first_gram = jnp.einsum("mpi,mpj->pij", grouped, grouped, precision=precise, preferred_element_type=jnp.float32)
    first_basis = jax.vmap(eigensolve)(first_gram)

    def second(position):
        prior_pair = jnp.maximum(position - 1, 0).astype(jnp.int32)
        later_pair = jnp.minimum(position + 1, N_PAIR - 1).astype(jnp.int32)
        upper_offset = jnp.where(position == 1, BLOCK, 0).astype(jnp.int32)
        lower_offset = jnp.where(position == N_PAIR - 1, 0, BLOCK).astype(jnp.int32)
        zero_index = jnp.zeros((), jnp.int32)
        upper_panel = lax.dynamic_slice(matrix, (zero_index, (prior_pair * pair_width).astype(jnp.int32)), (ROWS, pair_width))
        lower_panel = lax.dynamic_slice(matrix, (zero_index, (later_pair * pair_width).astype(jnp.int32)), (ROWS, pair_width))
        upper_cols = lax.dynamic_slice(first_basis[prior_pair], (zero_index, upper_offset), (pair_width, BLOCK))
        lower_cols = lax.dynamic_slice(first_basis[later_pair], (zero_index, lower_offset), (pair_width, BLOCK))
        upper_part = jnp.dot(upper_panel, upper_cols, precision=precise, preferred_element_type=jnp.float32)
        lower_part = jnp.dot(lower_panel, lower_cols, precision=precise, preferred_element_type=jnp.float32)
        gram_upper = panel_product(upper_part, upper_part)
        gram_cross = panel_product(upper_part, lower_part)
        gram_lower = panel_product(lower_part, lower_part)
        second_gram = jnp.concatenate([jnp.concatenate([gram_upper, gram_cross], axis=1), jnp.concatenate([gram_cross.T, gram_lower], axis=1)], axis=0)
        second_basis = eigensolve(second_gram)
        rotated = jnp.dot(upper_part, second_basis[:BLOCK], precision=precise, preferred_element_type=jnp.float32)
        rotated = rotated + jnp.dot(lower_part, second_basis[BLOCK:], precision=precise, preferred_element_type=jnp.float32)
        return jnp.abs(rotated), jnp.sum(rotated * rotated, axis=0) / ROWS

    stacked, energies = lax.map(second, jnp.arange(N_PAIR, dtype=jnp.int32))
    magnitudes = jnp.transpose(stacked, (1, 0, 2)).reshape(ROWS, COLS)
    return magnitudes, energies.reshape(COLS)
```

```python
import jax
import jax.numpy as jnp
import numpy as np
from jax import lax
from jax.experimental import pallas as pl
from jax.experimental.pallas import tpu as pltpu
from jax.sharding import PartitionSpec as P

STEPS = 16
HALF = 128
PACKED = HALF + 8
CHUNK = 512
f32 = jnp.float32
bf16 = jnp.bfloat16


def restore_table(order_size, step_count):
    labels = np.arange(order_size)
    middle = order_size // 2
    for number in range(step_count):
        labels = np.concatenate(
            [
                labels[0:1],
                labels[middle : middle + 1],
                labels[1 : middle - 1],
                labels[middle + 1 :],
                labels[middle - 1 : middle],
            ]
        )
    restore = np.argsort(labels)
    return np.eye(order_size, dtype=np.float32)[:, restore]


def split(value):
    high = value.astype(bf16)
    return high, (value - high.astype(f32)).astype(bf16)


def dot(left, right):
    return jnp.dot(left, right, preferred_element_type=f32)


def dot_rows(left, right):
    return lax.dot_general(left, right, (((0,), (0,)), ((), ())), preferred_element_type=f32)


def diagonal_mask():
    across = lax.broadcasted_iota(jnp.int32, (HALF, HALF), 1)
    down = lax.broadcasted_iota(jnp.int32, (HALF, HALF), 0)
    return across, down


def pack(gram, core, mine_ref, other_ref):
    across, down = diagonal_mask()
    first = gram[:HALF, :HALF]
    second = gram[HALF:, HALF:]
    cross = gram[:HALF, HALF:]
    square = jnp.where(down <= across, first, second)
    diagonal = jnp.sum(jnp.where(down == across, second, 0.0), axis=0, keepdims=True)
    keeps_square = core == 0
    mine_ref[:HALF] = jnp.where(keeps_square, square, cross)
    other_ref[:HALF] = jnp.where(keeps_square, cross, square)
    strip = jnp.broadcast_to(diagonal, (8, HALF))
    mine_ref[HALF:] = strip
    other_ref[HALF:] = strip


def unpack(core, mine, other, lead_ref, trail_ref):
    across, down = diagonal_mask()
    keeps_square = core == 0
    square = jnp.where(keeps_square, mine[:HALF], other[:HALF])
    cross = jnp.where(keeps_square, other[:HALF], mine[:HALF])
    diagonal = jnp.where(keeps_square, mine[HALF : HALF + 1], other[HALF : HALF + 1])
    flipped = square.T
    lead_ref[:HALF] = jnp.where(down <= across, square, flipped)
    lead_ref[HALF:] = cross.T
    trail_ref[:HALF] = cross
    second = jnp.where(down > across, square, flipped)
    trail_ref[HALF:] = jnp.where(down == across, diagonal, second)


def first_gram_kernel(flags_ref, panel_ref, mine_ref, other_ref, same_ref, mixed_ref):
    at = pl.program_id(0)
    high, low = split(panel_ref[...])
    same = dot_rows(high, high)
    mixed = dot_rows(high, low)

    @pl.when(at == 0)
    def _():
        same_ref[...] = same
        mixed_ref[...] = mixed

    @pl.when(at > 0)
    def _():
        same_ref[...] += same
        mixed_ref[...] += mixed

    @pl.when(at == pl.num_programs(0) - 1)
    def _():
        mixed = mixed_ref[...]
        pack(same_ref[...] + (mixed + mixed.T), flags_ref[0], mine_ref, other_ref)


def second_gram_kernel(
    flags_ref, top_ref, upper_ref, lower_ref, mine_ref, other_ref, same_ref, mixed_ref
):
    at = pl.program_id(0)
    upper = jnp.where(flags_ref[1] == 1, top_ref[...], upper_ref[...])
    lower = jnp.where(flags_ref[2] == 1, top_ref[...], lower_ref[...])
    high, low = split(jnp.concatenate([upper, lower], axis=1))
    same = dot_rows(high, high)
    mixed = dot_rows(high, low)

    @pl.when(at == 0)
    def _():
        same_ref[...] = same
        mixed_ref[...] = mixed

    @pl.when(at > 0)
    def _():
        same_ref[...] += same
        mixed_ref[...] += mixed

    @pl.when(at == pl.num_programs(0) - 1)
    def _():
        mixed = mixed_ref[...]
        pack(same_ref[...] + (mixed + mixed.T), flags_ref[0], mine_ref, other_ref)


def gram_outputs():
    shape = jax.ShapeDtypeStruct((PACKED, HALF), f32)
    spec = pl.BlockSpec((PACKED, HALF), lambda i, flags: (0, 0))
    scratch = pltpu.VMEM((2 * HALF, 2 * HALF), f32)
    return (shape, shape), (spec, spec), [scratch, scratch]


def first_gram(flags, panel):
    shapes, specs, scratch = gram_outputs()
    return pl.pallas_call(
        first_gram_kernel,
        out_shape=shapes,
        grid_spec=pltpu.PrefetchScalarGridSpec(
            num_scalar_prefetch=1,
            grid=(panel.shape[0] // CHUNK,),
            in_specs=[pl.BlockSpec((CHUNK, 2 * HALF), lambda i, flags: (i, 0))],
            out_specs=specs,
            scratch_shapes=scratch,
        ),
    )(flags, panel)


def second_gram(flags, top, upper, lower):
    shapes, specs, scratch = gram_outputs()
    block = (CHUNK, HALF)
    return pl.pallas_call(
        second_gram_kernel,
        out_shape=shapes,
        grid_spec=pltpu.PrefetchScalarGridSpec(
            num_scalar_prefetch=1,
            grid=(top.shape[0] // CHUNK,),
            in_specs=[
                pl.BlockSpec(block, lambda i, flags: (i * (flags[1] + flags[2]), 0)),
                pl.BlockSpec(block, lambda i, flags: (i, 0)),
                pl.BlockSpec(block, lambda i, flags: (i, 0)),
            ],
            out_specs=specs,
            scratch_shapes=scratch,
        ),
    )(flags, top, upper, lower)


def turn(leading, trailing, cos_row, sin_row, across):
    first = cos_row * leading - sin_row * trailing
    second = sin_row * leading + cos_row * trailing
    moved = pltpu.roll(jnp.where(across == 0, second, first), 1, 1)
    top = jnp.where(across == 0, first, moved)
    bottom = jnp.where(across == HALF - 1, first, pltpu.roll(second, HALF - 1, 1))
    return top, bottom


def half_angle(first, coupling, second):
    along = first - second
    up = -2.0 * coupling
    along_size = jnp.abs(along)
    up_size = jnp.abs(up)
    scale = jnp.maximum(along_size, up_size)
    flat = scale == 0.0
    inverse = 1.0 / jnp.where(flat, 1.0, scale)
    along_part = jnp.where(flat, 1.0, along_size * inverse)
    up_part = up_size * inverse
    length = lax.rsqrt(along_part * along_part + up_part * up_part)
    square = 0.5 + 0.5 * (along_part * length)
    root = lax.rsqrt(square)
    large = square * root
    small = 0.5 * (up_part * length) * root
    ahead = along >= 0.0
    cos_part = jnp.where(ahead, large, small)
    sin_part = jnp.where(ahead, small, large)
    return cos_part, jnp.where(up > 0.0, sin_part, -sin_part)


def diagonal_of(square, mask):
    return jnp.sum(jnp.where(mask, square, 0.0), axis=0, keepdims=True)


def eigensolve(lead_ref, trail_ref, basis_lead_ref, basis_trail_ref):
    across = lax.broadcasted_iota(jnp.int32, (2 * HALF, HALF), 1)
    down = lax.broadcasted_iota(jnp.int32, (2 * HALF, HALF), 0)
    mask = (across == down)[:HALF]
    basis_lead_ref[...] = jnp.where(across == down, 1.0, 0.0)
    basis_trail_ref[...] = jnp.where(across + HALF == down, 1.0, 0.0)

    def step(number, carried):
        cos_row, sin_row = half_angle(
            diagonal_of(lead_ref[:HALF], mask),
            diagonal_of(trail_ref[:HALF], mask),
            diagonal_of(trail_ref[HALF:], mask),
        )
        lead, trail = turn(lead_ref[...], trail_ref[...], cos_row, sin_row, across)
        lead, trail = turn(
            jnp.concatenate([lead[:HALF].T, trail[:HALF].T], axis=0),
            jnp.concatenate([lead[HALF:].T, trail[HALF:].T], axis=0),
            cos_row,
            sin_row,
            across,
        )
        lead_ref[...] = lead
        trail_ref[...] = trail
        lead, trail = turn(basis_lead_ref[...], basis_trail_ref[...], cos_row, sin_row, across)
        basis_lead_ref[...] = lead
        basis_trail_ref[...] = trail
        return carried

    lax.fori_loop(0, STEPS, step, 0)


def restored(value, table):
    return jnp.dot(value, table, precision=lax.Precision.HIGHEST, preferred_element_type=f32)


def first_round_kernel(
    flags_ref,
    mine_ref,
    other_ref,
    table_ref,
    panel_hbm,
    down_hbm,
    up_hbm,
    top_hbm,
    panel_ref,
    down_ref,
    up_ref,
    top_ref,
    lead_ref,
    trail_ref,
    basis_lead_ref,
    basis_trail_ref,
    in_sem,
    down_sems,
    up_sems,
    top_sem,
):
    is_first = flags_ref[1] == 1
    at_edge = flags_ref[1] + flags_ref[2] > 0
    fetch = pltpu.make_async_copy(panel_hbm, panel_ref, in_sem)
    fetch.start()
    unpack(flags_ref[0], mine_ref[...], other_ref[...], lead_ref, trail_ref)
    eigensolve(lead_ref, trail_ref, basis_lead_ref, basis_trail_ref)
    basis = jnp.concatenate([basis_lead_ref[...], basis_trail_ref[...]], axis=1)
    basis_high, basis_low = split(restored(basis, table_ref[...]))
    fetch.wait()
    copies = []
    for number in range(panel_ref.shape[0] // CHUNK):
        rows = pl.ds(number * CHUNK, CHUNK)
        high, low = split(panel_ref[rows])
        product = dot(high, basis_high) + (dot(high, basis_low) + dot(low, basis_high))
        down_ref[rows] = product[:, HALF:]
        up_ref[rows] = jnp.where(is_first, product[:, HALF:], product[:, :HALF])
        top_ref[rows] = product[:, :HALF]
        for source, target, sems in (
            (down_ref, down_hbm, down_sems),
            (up_ref, up_hbm, up_sems),
        ):
            copy = pltpu.make_async_copy(source.at[rows], target.at[rows], sems.at[number])
            copy.start()
            copies.append(copy)

    @pl.when(at_edge)
    def _():
        copy = pltpu.make_async_copy(top_ref, top_hbm, top_sem)
        copy.start()
        copy.wait()

    for copy in copies:
        copy.wait()


def solve_scratch():
    return [pltpu.VMEM((2 * HALF, HALF), f32)] * 4


def first_round(flags, mine, other, table, panel):
    rows = panel.shape[0]
    shape = jax.ShapeDtypeStruct((rows, HALF), f32)
    count = rows // CHUNK
    anywhere = pl.BlockSpec(memory_space=pl.ANY)
    vmem = pl.BlockSpec(memory_space=pltpu.VMEM)
    return pl.pallas_call(
        first_round_kernel,
        out_shape=(shape, shape, shape),
        in_specs=[pl.BlockSpec(memory_space=pltpu.SMEM), vmem, vmem, vmem, anywhere],
        out_specs=(anywhere, anywhere, anywhere),
        scratch_shapes=[
            pltpu.VMEM((rows, 2 * HALF), f32),
            pltpu.VMEM((rows, HALF), f32),
            pltpu.VMEM((rows, HALF), f32),
            pltpu.VMEM((rows, HALF), f32),
        ]
        + solve_scratch()
        + [
            pltpu.SemaphoreType.DMA(()),
            pltpu.SemaphoreType.DMA((count,)),
            pltpu.SemaphoreType.DMA((count,)),
            pltpu.SemaphoreType.DMA(()),
        ],
        compiler_params=pltpu.CompilerParams(vmem_limit_bytes=32 * 2**20),
    )(flags, mine, other, table, panel)


def second_round_kernel(
    flags_ref,
    mine_ref,
    other_ref,
    table_ref,
    top_hbm,
    upper_hbm,
    lower_hbm,
    magnitudes_hbm,
    energies_ref,
    upper_ref,
    lower_ref,
    out_ref,
    lead_ref,
    trail_ref,
    basis_lead_ref,
    basis_trail_ref,
    in_sems,
    out_sems,
):
    is_first = flags_ref[1] == 1
    is_last = flags_ref[2] == 1

    def fetch(swapped, usual, target, sem):
        @pl.when(swapped)
        def _():
            pltpu.make_async_copy(top_hbm, target, sem).start()

        @pl.when(jnp.logical_not(swapped))
        def _():
            pltpu.make_async_copy(usual, target, sem).start()

    fetch(is_first, upper_hbm, upper_ref, in_sems.at[0])
    fetch(is_last, lower_hbm, lower_ref, in_sems.at[1])
    unpack(flags_ref[0], mine_ref[...], other_ref[...], lead_ref, trail_ref)
    eigensolve(lead_ref, trail_ref, basis_lead_ref, basis_trail_ref)
    table = table_ref[...]
    across, down = diagonal_mask()
    mask = across == down
    squares = jnp.concatenate(
        [diagonal_of(lead_ref[:HALF], mask), diagonal_of(trail_ref[HALF:], mask)], axis=1
    )
    squares = restored(jnp.broadcast_to(squares, (8, 2 * HALF)), table)
    energies_ref[...] = squares * (1.0 / (8 * upper_ref.shape[0]))
    basis = jnp.concatenate([basis_lead_ref[...], basis_trail_ref[...]], axis=1)
    basis_high, basis_low = split(restored(basis, table))
    pltpu.make_async_copy(upper_hbm, upper_ref, in_sems.at[0]).wait()
    pltpu.make_async_copy(lower_hbm, lower_ref, in_sems.at[1]).wait()
    copies = []
    for number in range(upper_ref.shape[0] // CHUNK):
        rows = pl.ds(number * CHUNK, CHUNK)
        high, low = split(jnp.concatenate([upper_ref[rows], lower_ref[rows]], axis=1))
        product = dot(high, basis_high) + (dot(high, basis_low) + dot(low, basis_high))
        out_ref[rows] = jnp.abs(product)
        copy = pltpu.make_async_copy(
            out_ref.at[rows], magnitudes_hbm.at[rows], out_sems.at[number]
        )
        copy.start()
        copies.append(copy)
    for copy in copies:
        copy.wait()


def second_round(flags, mine, other, table, top, upper, lower):
    rows = top.shape[0]
    count = rows // CHUNK
    anywhere = pl.BlockSpec(memory_space=pl.ANY)
    vmem = pl.BlockSpec(memory_space=pltpu.VMEM)
    return pl.pallas_call(
        second_round_kernel,
        out_shape=(
            jax.ShapeDtypeStruct((rows, 2 * HALF), f32),
            jax.ShapeDtypeStruct((8, 2 * HALF), f32),
        ),
        in_specs=[pl.BlockSpec(memory_space=pltpu.SMEM), vmem, vmem, vmem]
        + [anywhere, anywhere, anywhere],
        out_specs=(anywhere, vmem),
        scratch_shapes=[
            pltpu.VMEM((rows, HALF), f32),
            pltpu.VMEM((rows, HALF), f32),
            pltpu.VMEM((rows, 2 * HALF), f32),
        ]
        + solve_scratch()
        + [pltpu.SemaphoreType.DMA((2,)), pltpu.SemaphoreType.DMA((count,))],
        compiler_params=pltpu.CompilerParams(vmem_limit_bytes=32 * 2**20),
    )(flags, mine, other, table, top, upper, lower)


def row_sum(mine, other):
    count = lax.axis_size("row")
    swap = [(at, at ^ 1) for at in range(count)]

    def shifted(value, chips):
        return lax.ppermute(
            value, "row", [(at, (at + 2 * chips) % count) for at in range(count)]
        )

    part = mine + lax.ppermute(other, "row", swap)
    across = shifted(part, 2)
    ahead = shifted(part, 1)
    behind = shifted(part, -1)
    part = (part + across) + (ahead + behind)
    return part, lax.ppermute(part, "row", swap)


def from_behind(value, axis, steps):
    count = lax.axis_size(axis)
    leading, last = (max(0, -steps), min(count, count - steps))
    return lax.ppermute(value, axis, [(source, source + steps) for source in range(leading, last)])


def body(matrix):
    position = lax.axis_index("pair")
    is_first = position == 0
    is_last = position == lax.axis_size("pair") - 1
    core = lax.axis_index("row") % 2
    flags = jnp.stack([core, is_first, is_last]).astype(jnp.int32)
    table = jnp.asarray(restore_table(2 * HALF, STEPS))
    mine, other = row_sum(*first_gram(flags, matrix))
    down, up, top = first_round(flags, mine, other, table, matrix)
    lower = from_behind(down, "pair", -1)
    upper = from_behind(up, "pair", 1)
    mine, other = row_sum(*second_gram(flags, top, upper, lower))
    magnitudes, energies = second_round(flags, mine, other, table, top, upper, lower)
    return magnitudes, energies[0]


def solution(mesh):
    return jax.shard_map(
        body,
        mesh=mesh,
        in_specs=(P("row", "pair"),),
        out_specs=(P("row", "pair"), P("pair")),
        check_vma=False,
    )
```

```python
import functools

import jax
import jax.numpy as jnp
import numpy as np
from jax import lax
from jax.experimental import pallas as pl
from jax.experimental.pallas import tpu as pltpu
from jax.sharding import PartitionSpec as P

STEPS = 16
HALF = 128
PACKED = HALF + 8
CHUNK = 512
CHUNKS = (2048, 1024, 1024)
f32 = jnp.float32
bf16 = jnp.bfloat16


def restore_table(order_size, step_count):
    labels = np.arange(order_size)
    middle = order_size // 2
    for number in range(step_count):
        labels = np.concatenate(
            [
                labels[0:1],
                labels[middle : middle + 1],
                labels[1 : middle - 1],
                labels[middle + 1 :],
                labels[middle - 1 : middle],
            ]
        )
    restore = np.argsort(labels)
    return np.eye(order_size, dtype=np.float32)[:, restore]


def split(value):
    high = value.astype(bf16)
    return high, (value - high.astype(f32)).astype(bf16)


def dot(left, right):
    return jnp.dot(left, right, preferred_element_type=f32)


def dot_rows(left, right):
    return lax.dot_general(left, right, (((0,), (0,)), ((), ())), preferred_element_type=f32)


def diagonal_mask():
    across = lax.broadcasted_iota(jnp.int32, (HALF, HALF), 1)
    down = lax.broadcasted_iota(jnp.int32, (HALF, HALF), 0)
    return across, down


def pack(gram, core, mine_ref, other_ref):
    across, down = diagonal_mask()
    first = gram[:HALF, :HALF]
    second = gram[HALF:, HALF:]
    cross = gram[:HALF, HALF:]
    square = jnp.where(down <= across, first, second)
    diagonal = jnp.sum(jnp.where(down == across, second, 0.0), axis=0, keepdims=True)
    keeps_square = core == 0
    mine_ref[:HALF] = jnp.where(keeps_square, square, cross)
    other_ref[:HALF] = jnp.where(keeps_square, cross, square)
    strip = jnp.broadcast_to(diagonal, (8, HALF))
    mine_ref[HALF:] = strip
    other_ref[HALF:] = strip


def unpack(core, mine, other, lead_ref, trail_ref):
    across, down = diagonal_mask()
    keeps_square = core == 0
    square = jnp.where(keeps_square, mine[:HALF], other[:HALF])
    cross = jnp.where(keeps_square, other[:HALF], mine[:HALF])
    diagonal = jnp.where(keeps_square, mine[HALF : HALF + 1], other[HALF : HALF + 1])
    flipped = square.T
    lead_ref[:HALF] = jnp.where(down <= across, square, flipped)
    lead_ref[HALF:] = cross.T
    trail_ref[:HALF] = cross
    second = jnp.where(down > across, square, flipped)
    trail_ref[HALF:] = jnp.where(down == across, diagonal, second)


def add_gram(total_ref, panel):
    high, low = split(panel)
    total_ref[...] += dot_rows(high, jnp.concatenate([high, low], axis=1))


def finish_gram(total_ref, mine_ref, other_ref):
    mixed = total_ref[:, 2 * HALF :]
    gram = total_ref[:, : 2 * HALF] + (mixed + mixed.T)
    pack(gram, lax.axis_index("row") % 2, mine_ref, other_ref)


def first_gram_kernel(panel_hbm, mine_ref, other_ref, panel_ref, total_ref, sems):
    copies = []
    for number in range(panel_hbm.shape[0] // CHUNK):
        rows = pl.ds(number * CHUNK, CHUNK)
        copy = pltpu.make_async_copy(panel_hbm.at[rows], panel_ref.at[rows], sems.at[number])
        copy.start()
        copies.append((rows, copy))
    total_ref[...] = jnp.zeros_like(total_ref)
    for rows, copy in copies:
        copy.wait()
        add_gram(total_ref, panel_ref[rows])
    finish_gram(total_ref, mine_ref, other_ref)


def second_panel(top_ref, upper_ref, lower_ref, rows):
    position = lax.axis_index("pair")
    top = top_ref[rows]
    upper = jnp.where(position == 0, top, upper_ref[rows])
    lower = jnp.where(position == lax.axis_size("pair") - 1, top, lower_ref[rows])
    return jnp.concatenate([upper, lower], axis=1)


def second_gram_kernel(is_first, is_last, *refs):
    before_ref = None
    if not is_first:
        before_ref, *refs = refs
    top_ref, upper_ref, lower_ref, *refs = refs
    if is_last:
        mine_ref, other_ref, *refs = refs
    (total_ref,) = refs
    if is_first:
        total_ref[...] = jnp.zeros_like(total_ref)
    else:
        total_ref[...] = before_ref[...]
    for number in range(upper_ref.shape[0] // CHUNK):
        rows = pl.ds(number * CHUNK, CHUNK)
        add_gram(total_ref, second_panel(top_ref, upper_ref, lower_ref, rows))
    if is_last:
        finish_gram(total_ref, mine_ref, other_ref)


VMEM = pltpu.VMEM
PACKED_PAIR = (VMEM((PACKED, HALF), f32),) * 2
TOTAL = VMEM((2 * HALF, 4 * HALF), f32)
IN_VMEM = pl.BlockSpec(memory_space=pltpu.VMEM)
IN_HBM = pl.BlockSpec(memory_space=pltpu.HBM)
DMA = pltpu.SemaphoreType.DMA


def in_vmem(*values):
    return [pltpu.with_memory_space_constraint(value, pltpu.VMEM) for value in values]


def in_hbm(value):
    return pltpu.with_memory_space_constraint(value, pltpu.HBM)


def params():
    return pltpu.CompilerParams(vmem_limit_bytes=16 * 2**20)


def cost(rows):
    return pl.CostEstimate(
        flops=2 * 3 * rows * 4 * HALF * HALF, bytes_accessed=16 * rows * HALF, transcendentals=0
    )


def first_gram(panel):
    rows = panel.shape[0]
    return pl.pallas_call(
        first_gram_kernel,
        out_shape=PACKED_PAIR + (VMEM(panel.shape, f32),),
        in_specs=[IN_HBM],
        out_specs=(IN_VMEM,) * 3,
        scratch_shapes=[TOTAL, DMA((rows // CHUNK,))],
        compiler_params=params(),
        cost_estimate=cost(rows),
    )(in_hbm(panel))


def second_gram(before, is_last, top, upper, lower):
    befores = [] if before is None else [before]
    operands = in_vmem(*befores, top, upper, lower)
    return pl.pallas_call(
        functools.partial(second_gram_kernel, before is None, is_last),
        out_shape=PACKED_PAIR if is_last else TOTAL,
        in_specs=[IN_VMEM] * len(operands),
        out_specs=(IN_VMEM, IN_VMEM) if is_last else IN_VMEM,
        scratch_shapes=[TOTAL] if is_last else [],
        compiler_params=params(),
        cost_estimate=cost(top.shape[0]),
    )(*operands)


def turn(leading, trailing, cos_row, sin_row, across):
    first = cos_row * leading - sin_row * trailing
    second = sin_row * leading + cos_row * trailing
    moved = pltpu.roll(jnp.where(across == 0, second, first), 1, 1)
    top = jnp.where(across == 0, first, moved)
    bottom = jnp.where(across == HALF - 1, first, pltpu.roll(second, HALF - 1, 1))
    return top, bottom


def half_angle(first, coupling, second):
    along = first - second
    up = -2.0 * coupling
    along_size = jnp.abs(along)
    up_size = jnp.abs(up)
    scale = jnp.maximum(along_size, up_size)
    flat = scale == 0.0
    inverse = 1.0 / jnp.where(flat, 1.0, scale)
    along_part = jnp.where(flat, 1.0, along_size * inverse)
    up_part = up_size * inverse
    length = lax.rsqrt(along_part * along_part + up_part * up_part)
    square = 0.5 + 0.5 * (along_part * length)
    root = lax.rsqrt(square)
    large = square * root
    small = 0.5 * (up_part * length) * root
    ahead = along >= 0.0
    cos_part = jnp.where(ahead, large, small)
    sin_part = jnp.where(ahead, small, large)
    return cos_part, jnp.where(up > 0.0, sin_part, -sin_part)


def eigensolve(lead_ref, trail_ref, basis_lead_ref, basis_trail_ref):
    across = lax.broadcasted_iota(jnp.int32, (2 * HALF, HALF), 1)
    down = lax.broadcasted_iota(jnp.int32, (2 * HALF, HALF), 0)
    mask = (across == down)[:HALF]
    basis_lead_ref[...] = jnp.where(across == down, 1.0, 0.0)
    basis_trail_ref[...] = jnp.where(across + HALF == down, 1.0, 0.0)

    def column_sums(value):
        return jnp.sum(value, axis=0, keepdims=True)

    def step(number, carried):
        cos_row, sin_row = half_angle(*carried)
        lead, trail = turn(lead_ref[...], trail_ref[...], cos_row, sin_row, across)
        lead_ref[...] = lead
        trail_ref[...] = trail
        basis_lead, basis_trail = turn(
            basis_lead_ref[...], basis_trail_ref[...], cos_row, sin_row, across
        )
        basis_lead_ref[...] = basis_lead
        basis_trail_ref[...] = basis_trail
        return (
            column_sums(basis_lead * lead),
            column_sums(basis_lead * trail),
            column_sums(basis_trail * trail),
        )

    def diagonal_of(square):
        return column_sums(jnp.where(mask, square, 0.0))

    first, _, second = lax.fori_loop(
        0,
        STEPS,
        step,
        (diagonal_of(lead_ref[:HALF]), diagonal_of(trail_ref[:HALF]), diagonal_of(trail_ref[HALF:])),
    )
    return jnp.concatenate([first, second], axis=1)


def restored_basis(basis_lead_ref, basis_trail_ref, table):
    basis = jnp.concatenate([basis_lead_ref[...], basis_trail_ref[...]], axis=1)
    high, low = split(basis)
    return dot(high, table).astype(bf16), dot(low, table).astype(bf16)


def product(panel, basis_high, basis_low):
    high, low = split(panel)
    return dot(high, basis_high) + (dot(high, basis_low) + dot(low, basis_high))


def first_round_kernel(mine_ref, other_ref, table_ref, panel_ref, *refs):
    outs, scratch = refs[: 3 * len(CHUNKS)], refs[3 * len(CHUNKS) :]
    unpack(lax.axis_index("row") % 2, mine_ref[...], other_ref[...], *scratch[:2])
    eigensolve(*scratch)
    basis = restored_basis(*scratch[2:], table_ref[...])
    is_first = lax.axis_index("pair") == 0
    start = 0
    for part, chunk in enumerate(CHUNKS):
        down_ref, up_ref, top_ref = outs[3 * part : 3 * part + 3]
        for number in range(chunk // CHUNK):
            rows = pl.ds(number * CHUNK, CHUNK)
            value = product(panel_ref[pl.ds(start + number * CHUNK, CHUNK)], *basis)
            down_ref[rows] = value[:, HALF:]
            up_ref[rows] = jnp.where(is_first, value[:, HALF:], value[:, :HALF])
            top_ref[rows] = value[:, :HALF]
        start += chunk


def solve_scratch():
    return [VMEM((2 * HALF, HALF), f32)] * 4


def first_round(mine, other, table, panel):
    return pl.pallas_call(
        first_round_kernel,
        out_shape=[VMEM((chunk, HALF), f32) for chunk in CHUNKS for _ in range(3)],
        in_specs=[IN_VMEM] * 4,
        out_specs=[IN_VMEM] * (3 * len(CHUNKS)),
        scratch_shapes=solve_scratch(),
        compiler_params=params(),
    )(*in_vmem(mine, other, table, panel))


def second_round_kernel(parts, *refs):
    mine_ref, other_ref, table_ref, *refs = refs
    sources, refs = refs[: 3 * parts], refs[3 * parts :]
    magnitudes_hbm, energies_ref, out_ref, *scratch, sems = refs
    unpack(lax.axis_index("row") % 2, mine_ref[...], other_ref[...], *scratch[:2])
    squares = eigensolve(*scratch)
    table = table_ref[...]
    basis = restored_basis(*scratch[2:], table)
    copies = []
    for part in range(parts):
        blocks = sources[3 * part : 3 * part + 3]
        for number in range(blocks[0].shape[0] // CHUNK):
            rows = pl.ds(len(copies) * CHUNK, CHUNK)
            panel = second_panel(*blocks, pl.ds(number * CHUNK, CHUNK))
            out_ref[rows] = jnp.abs(product(panel, *basis))
            copy = pltpu.make_async_copy(
                out_ref.at[rows], magnitudes_hbm.at[rows], sems.at[len(copies)]
            )
            copy.start()
            copies.append(copy)
    squares = jnp.dot(
        jnp.broadcast_to(squares, (8, 2 * HALF)),
        table.astype(f32),
        precision=lax.Precision.HIGHEST,
        preferred_element_type=f32,
    )
    total_rows = lax.axis_size("row") * out_ref.shape[0]
    energies_ref[...] = squares[:1] * (1.0 / total_rows)
    for copy in copies:
        copy.wait()


def second_round(mine, other, table, parts):
    rows = sum(part[0].shape[0] for part in parts)
    shape = (rows, 2 * HALF)
    operands = in_vmem(mine, other, table, *[value for part in parts for value in part])
    return pl.pallas_call(
        functools.partial(second_round_kernel, len(parts)),
        out_shape=(pltpu.HBM(shape, f32), jax.ShapeDtypeStruct((1, 2 * HALF), f32)),
        in_specs=[IN_VMEM] * len(operands),
        out_specs=(IN_HBM, IN_VMEM),
        scratch_shapes=[VMEM(shape, f32)] + solve_scratch() + [DMA((rows // CHUNK,))],
        compiler_params=params(),
    )(*operands)


def row_sum(mine, other):
    count = lax.axis_size("row")
    swap = [(at, at ^ 1) for at in range(count)]

    def shifted(value, chips):
        return lax.ppermute(
            value, "row", [(at, (at + 2 * chips) % count) for at in range(count)]
        )

    part = mine + lax.ppermute(other, "row", swap)
    across = shifted(part, 2)
    ahead = shifted(part, 1)
    behind = shifted(part, -1)
    part = (part + across) + (ahead + behind)
    return part, lax.ppermute(part, "row", swap)


def from_behind(value, axis, steps):
    count = lax.axis_size(axis)
    leading, last = (max(0, -steps), min(count, count - steps))
    return lax.ppermute(value, axis, [(source, source + steps) for source in range(leading, last)])


def body(matrix):
    table = jnp.asarray(restore_table(2 * HALF, STEPS), dtype=bf16)
    mine, other, panel = first_gram(matrix)
    blocks = first_round(*row_sum(mine, other), table, panel)
    parts = []
    for number in range(len(CHUNKS)):
        down, up, top = blocks[3 * number : 3 * number + 3]
        parts.append((top, from_behind(up, "pair", 1), from_behind(down, "pair", -1)))
    total = None
    for number, part in enumerate(parts):
        total = second_gram(total, number == len(parts) - 1, *part)
    magnitudes, energies = second_round(*row_sum(*total), table, parts)
    return magnitudes, energies.reshape(2 * HALF)


def solution(mesh):
    return jax.shard_map(
        body,
        mesh=mesh,
        in_specs=(P("row", "pair"),),
        out_specs=(P("row", "pair"), P("pair")),
        check_vma=False,
    )
```

```python
import functools

import jax
import jax.numpy as jnp
import numpy as np
from jax import lax
from jax.experimental import pallas as pl
from jax.experimental.pallas import tpu as pltpu
from jax.sharding import PartitionSpec as P

STEPS = 16
HALF = 128
REACH = 2 * STEPS - 1
CHUNK = 512
GRAM_CHUNK = 1024
CHUNKS = (2048, 1024, 1024)
f32 = jnp.float32
bf16 = jnp.bfloat16


def restore_table(order_size, step_count):
    labels = np.arange(order_size)
    middle = order_size // 2
    for number in range(step_count):
        labels = np.concatenate(
            [
                labels[0:1],
                labels[middle : middle + 1],
                labels[1 : middle - 1],
                labels[middle + 1 :],
                labels[middle - 1 : middle],
            ]
        )
    restore = np.argsort(labels)
    return np.eye(order_size, dtype=np.float32)[:, restore]


def split(value):
    high = value.astype(bf16)
    return high, (value - high.astype(f32)).astype(bf16)


def dot(left, right):
    return jnp.dot(left, right, preferred_element_type=f32)


def dot_rows(left, right):
    return lax.dot_general(left, right, (((0,), (0,)), ((), ())), preferred_element_type=f32)


def grid_of(rows):
    across = lax.broadcasted_iota(jnp.int32, (rows, HALF), 1)
    down = lax.broadcasted_iota(jnp.int32, (rows, HALF), 0)
    return across, down


def pack(gram, swapped, square_ref):
    first = jnp.where(swapped, gram[HALF:, HALF:], gram[:HALF, :HALF])
    second = jnp.where(swapped, gram[:HALF, :HALF], gram[HALF:, HALF:])
    cross = jnp.where(swapped, gram[HALF:, :HALF], gram[:HALF, HALF:])
    across, down = grid_of(HALF)
    ahead = (across - down) & (HALF - 1)
    square_ref[...] = jnp.where(
        jnp.logical_or(ahead < REACH, ahead > HALF - REACH),
        cross,
        jnp.where(
            ahead < 2 * REACH, pltpu.roll(first, REACH, 1), pltpu.roll(second, 2 * REACH, 1)
        ),
    )


def fold(value):
    return value[: HALF // 2] + value[HALF // 2 :]


def unfold(value):
    across, down = grid_of(HALF)
    near = jnp.abs(across - down) < HALF // 4
    return jnp.where(near, jnp.concatenate([value, value], axis=0), 0.0)


def unpack(square, lead_ref, trail_ref):
    across, down = grid_of(HALF)
    ahead = across - down

    def symmetric(moved):
        upper = pltpu.roll(square, HALF - moved, 1)
        upper = jnp.where(jnp.logical_and(ahead >= 0, ahead < REACH), upper, 0.0)
        return fold(jnp.where(ahead >= 0, upper, upper.T))

    cross = jnp.where(jnp.abs(ahead) < REACH, square, 0.0)
    lead_ref[: HALF // 2] = symmetric(REACH)
    lead_ref[HALF // 2 :] = fold(cross.T)
    trail_ref[: HALF // 2] = fold(cross)
    trail_ref[HALF // 2 :] = symmetric(2 * REACH)


def add_gram(total_ref, panel):
    high, low = split(panel)
    total_ref[...] += dot_rows(high, jnp.concatenate([high, low], axis=1))


def finish_gram(total_ref, swapped, square_ref):
    mixed = total_ref[:, 2 * HALF :]
    gram = total_ref[:, : 2 * HALF] + (mixed + mixed.T)
    pack(gram, swapped, square_ref)


def first_gram_kernel(panel_hbm, square_ref, panel_ref, total_ref, sems):
    copies = []
    for number in range(panel_hbm.shape[0] // GRAM_CHUNK):
        rows = pl.ds(number * GRAM_CHUNK, GRAM_CHUNK)
        copy = pltpu.make_async_copy(panel_hbm.at[rows], panel_ref.at[rows], sems.at[number])
        copy.start()
        copies.append((rows, copy))
    total_ref[...] = jnp.zeros_like(total_ref)
    for rows, copy in copies:
        copy.wait()
        add_gram(total_ref, panel_ref[rows])
    finish_gram(total_ref, False, square_ref)


def is_odd():
    return lax.axis_index("pair") % 2 == 1


def second_gram_kernel(is_first, is_last, *refs):
    before_ref = None
    if not is_first:
        before_ref, *refs = refs
    far_ref, near_ref, *refs = refs
    if is_last:
        square_ref, *refs = refs
    (total_ref,) = refs
    if is_first:
        total_ref[...] = jnp.zeros_like(total_ref)
    else:
        total_ref[...] = before_ref[...]
    for number in range(near_ref.shape[0] // GRAM_CHUNK):
        rows = pl.ds(number * GRAM_CHUNK, GRAM_CHUNK)
        add_gram(total_ref, jnp.concatenate([far_ref[rows], near_ref[rows]], axis=1))
    if is_last:
        finish_gram(total_ref, is_odd(), square_ref)


VMEM = pltpu.VMEM
SQUARE = VMEM((HALF, HALF), f32)
TOTAL = VMEM((2 * HALF, 4 * HALF), f32)
IN_VMEM = pl.BlockSpec(memory_space=pltpu.VMEM)
IN_HBM = pl.BlockSpec(memory_space=pltpu.HBM)
DMA = pltpu.SemaphoreType.DMA


def in_vmem(*values):
    return [pltpu.with_memory_space_constraint(value, pltpu.VMEM) for value in values]


def in_hbm(value):
    return pltpu.with_memory_space_constraint(value, pltpu.HBM)


def params():
    return pltpu.CompilerParams(vmem_limit_bytes=16 * 2**20)


def cost(rows):
    return pl.CostEstimate(
        flops=2 * 3 * rows * 4 * HALF * HALF, bytes_accessed=16 * rows * HALF, transcendentals=0
    )


def first_gram(panel):
    rows = panel.shape[0]
    return pl.pallas_call(
        first_gram_kernel,
        out_shape=(SQUARE, VMEM(panel.shape, f32)),
        in_specs=[IN_HBM],
        out_specs=(IN_VMEM, IN_VMEM),
        scratch_shapes=[TOTAL, DMA((rows // GRAM_CHUNK,))],
        compiler_params=params(),
        cost_estimate=cost(rows),
    )(in_hbm(panel))


def second_gram(before, is_last, far, near):
    befores = [] if before is None else [before]
    operands = in_vmem(*befores, far, near)
    return pl.pallas_call(
        functools.partial(second_gram_kernel, before is None, is_last),
        out_shape=SQUARE if is_last else TOTAL,
        in_specs=[IN_VMEM] * len(operands),
        out_specs=IN_VMEM,
        scratch_shapes=[TOTAL] if is_last else [],
        compiler_params=params(),
        cost_estimate=cost(near.shape[0]),
    )(*operands)


def rotate(leading, trailing, cos_row, sin_row):
    return cos_row * leading - sin_row * trailing, sin_row * leading + cos_row * trailing


def move(first, second, across):
    moved = pltpu.roll(jnp.where(across == 0, second, first), 1, 1)
    top = jnp.where(across == 0, first, moved)
    bottom = jnp.where(across == HALF - 1, first, pltpu.roll(second, HALF - 1, 1))
    return top, bottom


def half_angle(first, coupling, second):
    along = first - second
    up = -2.0 * coupling
    along_size = jnp.abs(along)
    up_size = jnp.abs(up)
    scale = jnp.maximum(along_size, up_size)
    flat = scale == 0.0
    inverse = 1.0 / jnp.where(flat, 1.0, scale)
    along_part = jnp.where(flat, 1.0, along_size * inverse)
    up_part = up_size * inverse
    length = lax.rsqrt(along_part * along_part + up_part * up_part)
    square = 0.5 + 0.5 * (along_part * length)
    root = lax.rsqrt(square)
    large = square * root
    small = 0.5 * (up_part * length) * root
    ahead = along >= 0.0
    cos_part = jnp.where(ahead, large, small)
    sin_part = jnp.where(ahead, small, large)
    return cos_part, jnp.where(up > 0.0, sin_part, -sin_part)


def eigensolve(lead_ref, trail_ref, basis_lead_ref, basis_trail_ref):
    across, down = grid_of(HALF)
    half = HALF // 2
    mask = jnp.logical_and((across & (half - 1)) == (down & (half - 1)), down < half)
    basis_lead_ref[...] = jnp.where(mask, 1.0, 0.0)
    basis_trail_ref[...] = jnp.where(
        jnp.logical_and((across & (half - 1)) == (down & (half - 1)), down >= half), 1.0, 0.0
    )

    def column_sums(value):
        return jnp.sum(value, axis=0, keepdims=True)

    def step(number, carried):
        turns = half_angle(*carried)
        product = rotate(lead_ref[...], trail_ref[...], *turns)
        basis = rotate(basis_lead_ref[...], basis_trail_ref[...], *turns)
        first, second = move(
            column_sums(product[0] * basis[0]), column_sums(product[1] * basis[1]), across[:1]
        )
        lead_ref[...], trail = move(*product, across)
        trail_ref[...] = trail
        basis_lead, basis_trail_ref[...] = move(*basis, across)
        basis_lead_ref[...] = basis_lead
        return first, column_sums(basis_lead * trail), second

    def diagonal_of(folded):
        return column_sums(jnp.where(mask[:half], folded, 0.0))

    first, _, second = lax.fori_loop(
        0,
        STEPS,
        step,
        (diagonal_of(lead_ref[:half]), diagonal_of(trail_ref[:half]), diagonal_of(trail_ref[half:])),
        unroll=4,
    )
    return jnp.concatenate([first, second], axis=1)


def restored_basis(basis_lead_ref, basis_trail_ref, table):
    half = HALF // 2
    basis = jnp.concatenate(
        [
            jnp.concatenate([unfold(ref[:half]), unfold(ref[half:])], axis=0)
            for ref in (basis_lead_ref, basis_trail_ref)
        ],
        axis=1,
    )
    high, low = split(basis)
    return dot(high, table).astype(bf16), dot(low, table).astype(bf16)


def product(panel, basis_high, basis_low):
    high, low = split(panel)
    return dot(high, basis_high) + (dot(high, basis_low) + dot(low, basis_high))


def project(panel_ref, basis, start, near_ref, far_ref):
    for number in range(near_ref.shape[0] // CHUNK):
        rows = pl.ds(number * CHUNK, CHUNK)
        value = product(panel_ref[pl.ds(start + number * CHUNK, CHUNK)], *basis)
        near_ref[rows] = value[:, :HALF]
        far_ref[rows] = value[:, HALF:]


def first_round_kernel(
    *refs,
):
    *parts, table_ref, panel_ref, near_ref, far_ref, high_ref, low_ref = refs[:10]
    scratch = refs[10:]
    unpack(total_of(parts), *scratch[:2])
    eigensolve(*scratch)
    swapped = jnp.logical_or(lax.axis_index("pair") == 0, is_odd())
    basis = [
        jnp.where(swapped, jnp.concatenate([value[:, HALF:], value[:, :HALF]], axis=1), value)
        for value in restored_basis(*scratch[2:], table_ref[...])
    ]
    project(panel_ref, basis, 0, near_ref, far_ref)
    high_ref[...], low_ref[...] = basis


def later_rows_kernel(high_ref, low_ref, panel_ref, *outs):
    start = CHUNKS[0]
    for part in range(0, len(outs), 2):
        project(panel_ref, (high_ref[...], low_ref[...]), start, *outs[part : part + 2])
        start += outs[part].shape[0]


def solve_scratch():
    return [VMEM((HALF, HALF), f32)] * 4


def first_round(sums, table, panel):
    basis = VMEM((2 * HALF, 2 * HALF), bf16)
    near, far, high, low = pl.pallas_call(
        first_round_kernel,
        out_shape=[VMEM((CHUNKS[0], HALF), f32)] * 2 + [basis] * 2,
        in_specs=[IN_VMEM] * 6,
        out_specs=[IN_VMEM] * 4,
        scratch_shapes=solve_scratch(),
        compiler_params=params(),
    )(*in_vmem(*sums, table, panel))
    later = pl.pallas_call(
        later_rows_kernel,
        out_shape=[VMEM((chunk, HALF), f32) for chunk in CHUNKS[1:] for _ in range(2)],
        in_specs=[IN_VMEM] * 3,
        out_specs=[IN_VMEM] * (2 * len(CHUNKS) - 2),
        compiler_params=params(),
        cost_estimate=cost(sum(CHUNKS[1:])),
    )(*in_vmem(high, low, panel))
    return [near, far] + list(later)


def second_round_kernel(parts, *refs):
    parts_of_sum, (table_ref, *refs) = refs[:4], refs[4:]
    sources, refs = refs[: 2 * parts], refs[2 * parts :]
    magnitudes_hbm, energies_ref, out_ref, *scratch, sems = refs
    unpack(total_of(parts_of_sum), *scratch[:2])
    squares = eigensolve(*scratch)
    table = table_ref[...]
    basis = [
        jnp.where(is_odd(), jnp.concatenate([value[HALF:], value[:HALF]], axis=0), value)
        for value in restored_basis(*scratch[2:], table)
    ]
    copies = []
    for part in range(parts):
        far_ref, near_ref = sources[2 * part : 2 * part + 2]
        for number in range(near_ref.shape[0] // CHUNK):
            rows = pl.ds(len(copies) * CHUNK, CHUNK)
            source = pl.ds(number * CHUNK, CHUNK)
            panel = jnp.concatenate([far_ref[source], near_ref[source]], axis=1)
            out_ref[rows] = jnp.abs(product(panel, *basis))
            copy = pltpu.make_async_copy(
                out_ref.at[rows], magnitudes_hbm.at[rows], sems.at[len(copies)]
            )
            copy.start()
            copies.append(copy)
    squares = jnp.dot(
        jnp.broadcast_to(squares, (8, 2 * HALF)),
        table.astype(f32),
        precision=lax.Precision.HIGHEST,
        preferred_element_type=f32,
    )
    total_rows = lax.axis_size("row") * out_ref.shape[0]
    energies_ref[...] = squares[:1] * (1.0 / total_rows)
    for copy in copies:
        copy.wait()


def second_round(sums, table, parts):
    rows = sum(part[0].shape[0] for part in parts)
    shape = (rows, 2 * HALF)
    operands = in_vmem(*sums, table, *[value for part in parts for value in part])
    return pl.pallas_call(
        functools.partial(second_round_kernel, len(parts)),
        out_shape=(pltpu.HBM(shape, f32), jax.ShapeDtypeStruct((1, 2 * HALF), f32)),
        in_specs=[IN_VMEM] * len(operands),
        out_specs=(IN_HBM, IN_VMEM),
        scratch_shapes=[VMEM(shape, f32)] + solve_scratch() + [DMA((rows // CHUNK,))],
        compiler_params=params(),
    )(*operands)


def row_sum(square):
    count = lax.axis_size("row")

    def shifted(value, chips):
        return lax.ppermute(value, "row", [(at, (at + 2 * chips) % count) for at in range(count)])

    square = square + lax.ppermute(square, "row", [(at, at ^ 1) for at in range(count)])
    return shifted(square, 1), shifted(square, -1), square, shifted(square, 2)


def total_of(parts):
    ahead, behind, own, across = [part[...] for part in parts]
    return (ahead + behind) + (own + across)


def exchange(near, far):
    last = lax.axis_size("pair") - 1
    inner = [(at, at - 1 + 2 * (at % 2)) for at in range(1, last)]
    return (
        lax.ppermute(far, "pair", [(0, 0)] + inner + [(last, last)]),
        lax.ppermute(near, "pair", [(at, at ^ 1) for at in range(last + 1)]),
    )


def body(matrix):
    table = jnp.asarray(restore_table(2 * HALF, STEPS), dtype=bf16)
    square, panel = first_gram(matrix)
    blocks = first_round(row_sum(square), table, panel)
    parts = [exchange(*blocks[at : at + 2]) for at in range(0, len(blocks), 2)]
    total = None
    for number, part in enumerate(parts):
        total = second_gram(total, number == len(parts) - 1, *part)
    magnitudes, energies = second_round(row_sum(total), table, parts)
    return magnitudes, energies.reshape(2 * HALF)


def solution(mesh):
    return jax.shard_map(
        body,
        mesh=mesh,
        in_specs=(P("row", "pair"),),
        out_specs=(P("row", "pair"), P("pair")),
        check_vma=False,
    )
```

```python
import functools

import jax
import jax.numpy as jnp
import numpy as np
from jax import lax
from jax.experimental import pallas as pl
from jax.experimental.pallas import tpu as pltpu
from jax.sharding import PartitionSpec as P

STEPS = 16
HALF = 128
SPAN = 2 * STEPS
REACH = SPAN - 1
CHUNK = 512
GRAM_CHUNK = 1024
CHUNKS = (1024, 1024, 1024, 1024)
f32 = jnp.float32
bf16 = jnp.bfloat16


def restore_table(order_size, step_count):
    labels = np.arange(order_size)
    middle = order_size // 2
    for number in range(step_count):
        labels = np.concatenate(
            [
                labels[0:1],
                labels[middle : middle + 1],
                labels[1 : middle - 1],
                labels[middle + 1 :],
                labels[middle - 1 : middle],
            ]
        )
    restore = np.argsort(labels)
    return np.eye(order_size, dtype=np.float32)[:, restore]


def split(value):
    high = value.astype(bf16)
    return high, (value - high.astype(f32)).astype(bf16)


def dot(left, right):
    return jnp.dot(left, right, preferred_element_type=f32)


def dot_rows(left, right):
    return lax.dot_general(left, right, (((0,), (0,)), ((), ())), preferred_element_type=f32)


def grid_of(rows):
    across = lax.broadcasted_iota(jnp.int32, (rows, HALF), 1)
    down = lax.broadcasted_iota(jnp.int32, (rows, HALF), 0)
    return across, down


def pack(total_ref, swapped, square_ref):
    def block(row, column):
        rows, columns = pl.ds(row * HALF, HALF), pl.ds(column * HALF, HALF)
        mixed = total_ref[rows, pl.ds((2 + column) * HALF, HALF)]
        turned = total_ref[columns, pl.ds((2 + row) * HALF, HALF)].T
        return total_ref[rows, columns] + (mixed + turned)

    first, second, cross = block(0, 0), block(1, 1), block(0, 1)
    if swapped is not None:
        first, second = jnp.where(swapped, second, first), jnp.where(swapped, first, second)
        cross = jnp.where(swapped, cross.T, cross)
    across, down = grid_of(HALF)
    ahead = (across - down) & (HALF - 1)
    square = jnp.where(
        jnp.logical_or(ahead < REACH, ahead > HALF - REACH),
        cross,
        jnp.where(ahead < 2 * SPAN, pltpu.roll(first, SPAN, 1), pltpu.roll(second, 2 * SPAN, 1)),
    )
    square_ref[:SPAN] = square[:SPAN]
    square_ref[SPAN : 2 * SPAN] = jnp.where(
        (ahead[:SPAN] & 1) == 0,
        square[SPAN : 2 * SPAN],
        pltpu.roll(square[2 * SPAN : 3 * SPAN], 1, 1),
    )
    square_ref[2 * SPAN :] = square[3 * SPAN :]


def fold(value):
    return value[: HALF // 2] + value[HALF // 2 :]


def unfold(value):
    across, down = grid_of(HALF)
    near = jnp.abs(across - down) < HALF // 4
    return jnp.where(near, jnp.concatenate([value, value], axis=0), 0.0)


def unpack(packed, lead_ref, trail_ref):
    across, down = grid_of(HALF)
    ahead = across - down
    even = (ahead[:SPAN] & 1) == 0
    shared = packed[SPAN : 2 * SPAN]
    square = jnp.concatenate(
        [
            packed[:SPAN],
            jnp.where(even, shared, 0.0),
            pltpu.roll(jnp.where(even, 0.0, shared), HALF - 1, 1),
            packed[2 * SPAN :],
        ],
        axis=0,
    )

    def symmetric(moved):
        upper = pltpu.roll(square, HALF - moved, 1)
        upper = jnp.where(jnp.logical_and(ahead >= 0, ahead < REACH), upper, 0.0)
        return fold(jnp.where(ahead >= 0, upper, upper.T))

    cross = jnp.where(jnp.abs(ahead) < REACH, square, 0.0)
    lead_ref[: HALF // 2] = symmetric(SPAN)
    lead_ref[HALF // 2 :] = fold(cross.T)
    trail_ref[: HALF // 2] = fold(cross)
    trail_ref[HALF // 2 :] = symmetric(2 * SPAN)


def add_gram(total_ref, panel):
    high, low = split(panel)
    total_ref[...] += dot_rows(high, jnp.concatenate([high, low], axis=1))


def first_gram_kernel(panel_hbm, square_ref, panel_ref, total_ref, sems):
    copies = []
    for number in range(panel_hbm.shape[0] // GRAM_CHUNK):
        rows = pl.ds(number * GRAM_CHUNK, GRAM_CHUNK)
        copy = pltpu.make_async_copy(panel_hbm.at[rows], panel_ref.at[rows], sems.at[number])
        copy.start()
        copies.append((rows, copy))
    total_ref[...] = jnp.zeros_like(total_ref)
    for rows, copy in copies:
        copy.wait()
        add_gram(total_ref, panel_ref[rows])
    pack(total_ref, None, square_ref)


def is_odd():
    return lax.axis_index("pair") % 2 == 1


def second_gram_kernel(is_first, is_last, *refs):
    before_ref = None
    if not is_first:
        before_ref, *refs = refs
    far_ref, near_ref, *refs = refs
    if is_last:
        square_ref, *refs = refs
    (total_ref,) = refs
    if is_first:
        total_ref[...] = jnp.zeros_like(total_ref)
    else:
        total_ref[...] = before_ref[...]
    for number in range(near_ref.shape[0] // GRAM_CHUNK):
        rows = pl.ds(number * GRAM_CHUNK, GRAM_CHUNK)
        add_gram(total_ref, jnp.concatenate([far_ref[rows], near_ref[rows]], axis=1))
    if is_last:
        pack(total_ref, is_odd(), square_ref)


VMEM = pltpu.VMEM
SQUARE = VMEM((3 * SPAN, HALF), f32)
TOTAL = VMEM((2 * HALF, 4 * HALF), f32)
IN_VMEM = pl.BlockSpec(memory_space=pltpu.VMEM)
IN_HBM = pl.BlockSpec(memory_space=pltpu.HBM)
DMA = pltpu.SemaphoreType.DMA


def in_vmem(*values):
    return [pltpu.with_memory_space_constraint(value, pltpu.VMEM) for value in values]


def in_hbm(value):
    return pltpu.with_memory_space_constraint(value, pltpu.HBM)


def params():
    return pltpu.CompilerParams(vmem_limit_bytes=16 * 2**20)


def cost(rows):
    return pl.CostEstimate(
        flops=2 * 3 * rows * 4 * HALF * HALF, bytes_accessed=16 * rows * HALF, transcendentals=0
    )


def first_gram(panel):
    rows = panel.shape[0]
    return pl.pallas_call(
        first_gram_kernel,
        out_shape=(SQUARE, VMEM(panel.shape, f32)),
        in_specs=[IN_HBM],
        out_specs=(IN_VMEM, IN_VMEM),
        scratch_shapes=[TOTAL, DMA((rows // GRAM_CHUNK,))],
        compiler_params=params(),
        cost_estimate=cost(rows),
    )(in_hbm(panel))


def second_gram(before, is_last, far, near):
    befores = [] if before is None else [before]
    operands = in_vmem(*befores, far, near)
    return pl.pallas_call(
        functools.partial(second_gram_kernel, before is None, is_last),
        out_shape=SQUARE if is_last else TOTAL,
        in_specs=[IN_VMEM] * len(operands),
        out_specs=IN_VMEM,
        scratch_shapes=[TOTAL] if is_last else [],
        compiler_params=params(),
        cost_estimate=cost(near.shape[0]),
    )(*operands)


def rotate(leading, trailing, cos_row, sin_row):
    return cos_row * leading - sin_row * trailing, sin_row * leading + cos_row * trailing


def move(first, second, across):
    moved = pltpu.roll(jnp.where(across == 0, second, first), 1, 1)
    top = jnp.where(across == 0, first, moved)
    bottom = jnp.where(across == HALF - 1, first, pltpu.roll(second, HALF - 1, 1))
    return top, bottom


def half_angle(first, coupling, second):
    along = first - second
    up = -2.0 * coupling
    along_size = jnp.abs(along)
    up_size = jnp.abs(up)
    scale = jnp.maximum(along_size, up_size)
    flat = scale == 0.0
    inverse = pl.reciprocal(jnp.where(flat, 1.0, scale), approx=True)
    along_part = jnp.where(flat, 1.0, along_size * inverse)
    up_part = up_size * inverse
    length = lax.rsqrt(along_part * along_part + up_part * up_part)
    square = 0.5 + 0.5 * (along_part * length)
    root = lax.rsqrt(square)
    large = square * root
    small = 0.5 * (up_part * length) * root
    ahead = along >= 0.0
    cos_part = jnp.where(ahead, large, small)
    sin_part = jnp.where(ahead, small, large)
    return cos_part, jnp.where(up > 0.0, sin_part, -sin_part)


def eigensolve(lead_ref, trail_ref, basis_lead_ref, basis_trail_ref):
    across, down = grid_of(HALF)
    half = HALF // 2
    mask = jnp.logical_and((across & (half - 1)) == (down & (half - 1)), down < half)
    basis_lead_ref[...] = jnp.where(mask, 1.0, 0.0)
    basis_trail_ref[...] = jnp.where(
        jnp.logical_and((across & (half - 1)) == (down & (half - 1)), down >= half), 1.0, 0.0
    )

    def column_sums(value):
        return jnp.sum(value, axis=0, keepdims=True)

    def step(number, carried):
        turns = half_angle(*carried)
        product = rotate(lead_ref[...], trail_ref[...], *turns)
        basis = rotate(basis_lead_ref[...], basis_trail_ref[...], *turns)
        first, second = move(
            column_sums(product[0] * basis[0]), column_sums(product[1] * basis[1]), across[:1]
        )
        lead_ref[...], trail = move(*product, across)
        trail_ref[...] = trail
        basis_lead, basis_trail_ref[...] = move(*basis, across)
        basis_lead_ref[...] = basis_lead
        return first, column_sums(basis_lead * trail), second

    def diagonal_of(folded):
        return column_sums(jnp.where(mask[:half], folded, 0.0))

    first, _, second = lax.fori_loop(
        0,
        STEPS,
        step,
        (diagonal_of(lead_ref[:half]), diagonal_of(trail_ref[:half]), diagonal_of(trail_ref[half:])),
        unroll=4,
    )
    return jnp.concatenate([first, second], axis=1)


def restored_basis(basis_lead_ref, basis_trail_ref, table):
    half = HALF // 2
    basis = jnp.concatenate(
        [
            jnp.concatenate([unfold(ref[:half]), unfold(ref[half:])], axis=0)
            for ref in (basis_lead_ref, basis_trail_ref)
        ],
        axis=1,
    )
    high, low = split(basis)
    return dot(high, table).astype(bf16), dot(low, table).astype(bf16)


def product(panel, basis_high, basis_low):
    high, low = split(panel)
    return dot(high, basis_high) + (dot(high, basis_low) + dot(low, basis_high))


def project(panel_ref, basis, start, near_ref, far_ref):
    for number in range(near_ref.shape[0] // CHUNK):
        rows = pl.ds(number * CHUNK, CHUNK)
        value = product(panel_ref[pl.ds(start + number * CHUNK, CHUNK)], *basis)
        near_ref[rows] = value[:, :HALF]
        far_ref[rows] = value[:, HALF:]


def first_round_kernel(
    *refs,
):
    *parts, table_ref, panel_ref, near_ref, far_ref, high_ref, low_ref = refs[:10]
    scratch = refs[10:]
    unpack(total_of(parts), *scratch[:2])
    eigensolve(*scratch)
    swapped = jnp.logical_or(lax.axis_index("pair") == 0, is_odd())
    basis = [
        jnp.where(swapped, jnp.concatenate([value[:, HALF:], value[:, :HALF]], axis=1), value)
        for value in restored_basis(*scratch[2:], table_ref[...])
    ]
    project(panel_ref, basis, 0, near_ref, far_ref)
    high_ref[...], low_ref[...] = basis


def later_rows_kernel(high_ref, low_ref, panel_ref, *outs):
    start = CHUNKS[0]
    for part in range(0, len(outs), 2):
        project(panel_ref, (high_ref[...], low_ref[...]), start, *outs[part : part + 2])
        start += outs[part].shape[0]


def solve_scratch():
    return [VMEM((HALF, HALF), f32)] * 4


def first_round(sums, table, panel):
    basis = VMEM((2 * HALF, 2 * HALF), bf16)
    near, far, high, low = pl.pallas_call(
        first_round_kernel,
        out_shape=[VMEM((CHUNKS[0], HALF), f32)] * 2 + [basis] * 2,
        in_specs=[IN_VMEM] * 6,
        out_specs=[IN_VMEM] * 4,
        scratch_shapes=solve_scratch(),
        compiler_params=params(),
    )(*in_vmem(*sums, table, panel))
    later = pl.pallas_call(
        later_rows_kernel,
        out_shape=[VMEM((chunk, HALF), f32) for chunk in CHUNKS[1:] for _ in range(2)],
        in_specs=[IN_VMEM] * 3,
        out_specs=[IN_VMEM] * (2 * len(CHUNKS) - 2),
        compiler_params=params(),
        cost_estimate=cost(sum(CHUNKS[1:])),
    )(*in_vmem(high, low, panel))
    return [near, far] + list(later)


def second_round_kernel(parts, *refs):
    parts_of_sum, (table_ref, *refs) = refs[:4], refs[4:]
    sources, refs = refs[: 2 * parts], refs[2 * parts :]
    magnitudes_hbm, energies_ref, out_ref, *scratch, sems = refs
    unpack(total_of(parts_of_sum), *scratch[:2])
    squares = eigensolve(*scratch)
    table = table_ref[...]
    basis = [
        jnp.where(is_odd(), jnp.concatenate([value[HALF:], value[:HALF]], axis=0), value)
        for value in restored_basis(*scratch[2:], table)
    ]
    copies = []
    for part in range(parts):
        far_ref, near_ref = sources[2 * part : 2 * part + 2]
        for number in range(near_ref.shape[0] // CHUNK):
            rows = pl.ds(len(copies) * CHUNK, CHUNK)
            source = pl.ds(number * CHUNK, CHUNK)
            panel = jnp.concatenate([far_ref[source], near_ref[source]], axis=1)
            out_ref[rows] = jnp.abs(product(panel, *basis))
            copy = pltpu.make_async_copy(
                out_ref.at[rows], magnitudes_hbm.at[rows], sems.at[len(copies)]
            )
            copy.start()
            copies.append(copy)
    squares = jnp.dot(
        jnp.broadcast_to(squares, (8, 2 * HALF)),
        table.astype(f32),
        precision=lax.Precision.HIGHEST,
        preferred_element_type=f32,
    )
    total_rows = lax.axis_size("row") * out_ref.shape[0]
    energies_ref[...] = squares[:1] * (1.0 / total_rows)
    for copy in copies:
        copy.wait()


def second_round(sums, table, parts):
    rows = sum(part[0].shape[0] for part in parts)
    shape = (rows, 2 * HALF)
    operands = in_vmem(*sums, table, *[value for part in parts for value in part])
    return pl.pallas_call(
        functools.partial(second_round_kernel, len(parts)),
        out_shape=(pltpu.HBM(shape, f32), jax.ShapeDtypeStruct((1, 2 * HALF), f32)),
        in_specs=[IN_VMEM] * len(operands),
        out_specs=(IN_HBM, IN_VMEM),
        scratch_shapes=[VMEM(shape, f32)] + solve_scratch() + [DMA((rows // CHUNK,))],
        compiler_params=params(),
    )(*operands)


def row_sum(square):
    count = lax.axis_size("row")

    def shifted(value, chips):
        return lax.ppermute(value, "row", [(at, (at + 2 * chips) % count) for at in range(count)])

    square = square + lax.ppermute(square, "row", [(at, at ^ 1) for at in range(count)])
    return shifted(square, 1), shifted(square, -1), square, shifted(square, 2)


def total_of(parts):
    ahead, behind, own, across = [part[...] for part in parts]
    return (ahead + behind) + (own + across)


def exchange(near, far):
    last = lax.axis_size("pair") - 1
    inner = [(at, at - 1 + 2 * (at % 2)) for at in range(1, last)]
    return (
        lax.ppermute(far, "pair", [(0, 0)] + inner + [(last, last)]),
        lax.ppermute(near, "pair", [(at, at ^ 1) for at in range(last + 1)]),
    )


def body(matrix):
    table = jnp.asarray(restore_table(2 * HALF, STEPS), dtype=bf16)
    square, panel = first_gram(matrix)
    blocks = first_round(row_sum(square), table, panel)
    parts = [exchange(*blocks[at : at + 2]) for at in range(0, len(blocks), 2)]
    total = None
    for number, part in enumerate(parts):
        total = second_gram(total, number == len(parts) - 1, *part)
    magnitudes, energies = second_round(row_sum(total), table, parts)
    return magnitudes, energies.reshape(2 * HALF)


def solution(mesh):
    return jax.shard_map(
        body,
        mesh=mesh,
        in_specs=(P("row", "pair"),),
        out_specs=(P("row", "pair"), P("pair")),
        check_vma=False,
    )
```

```python
import functools

import jax
import jax.numpy as jnp
import numpy as np
from jax import lax
from jax.experimental import pallas as pl
from jax.experimental.pallas import tpu as pltpu
from jax.sharding import PartitionSpec as P

STEPS = 16
HALF = 128
SPAN = 2 * STEPS
REACH = SPAN - 1
CHUNK = 512
GRAM_CHUNK = 1024
CHUNKS = (1024, 1024, 1536, 512)
f32 = jnp.float32
bf16 = jnp.bfloat16


def restore_table(order_size, step_count):
    labels = np.arange(order_size)
    middle = order_size // 2
    for number in range(step_count):
        labels = np.concatenate(
            [
                labels[0:1],
                labels[middle : middle + 1],
                labels[1 : middle - 1],
                labels[middle + 1 :],
                labels[middle - 1 : middle],
            ]
        )
    restore = np.argsort(labels)
    return np.eye(order_size, dtype=np.float32)[:, restore]


def split(value):
    high = value.astype(bf16)
    return high, (value - high.astype(f32)).astype(bf16)


def dot(left, right):
    return jnp.dot(left, right, preferred_element_type=f32)


def dot_rows(left, right):
    return lax.dot_general(left, right, (((0,), (0,)), ((), ())), preferred_element_type=f32)


def grid_of(rows):
    across = lax.broadcasted_iota(jnp.int32, (rows, HALF), 1)
    down = lax.broadcasted_iota(jnp.int32, (rows, HALF), 0)
    return across, down


def pack(total_ref, swapped, square_ref):
    def block(row, column):
        rows, columns = pl.ds(row * HALF, HALF), pl.ds(column * HALF, HALF)
        mixed = total_ref[rows, pl.ds((2 + column) * HALF, HALF)]
        turned = total_ref[columns, pl.ds((2 + row) * HALF, HALF)].T
        return total_ref[rows, columns] + (mixed + turned)

    first, second, cross = block(0, 0), block(1, 1), block(0, 1)
    if swapped is not None:
        first, second = jnp.where(swapped, second, first), jnp.where(swapped, first, second)
        cross = jnp.where(swapped, cross.T, cross)
    across, down = grid_of(HALF)
    ahead = (across - down) & (HALF - 1)
    square = jnp.where(
        jnp.logical_or(ahead < REACH, ahead > HALF - REACH),
        cross,
        jnp.where(ahead < 2 * SPAN, pltpu.roll(first, SPAN, 1), pltpu.roll(second, 2 * SPAN, 1)),
    )
    square_ref[:SPAN] = square[:SPAN]
    square_ref[SPAN : 2 * SPAN] = jnp.where(
        (ahead[:SPAN] & 1) == 0,
        square[SPAN : 2 * SPAN],
        pltpu.roll(square[2 * SPAN : 3 * SPAN], 1, 1),
    )
    square_ref[2 * SPAN :] = square[3 * SPAN :]


def fold(value):
    return value[: HALF // 2] + value[HALF // 2 :]


def unfold(value):
    across, down = grid_of(HALF)
    near = jnp.abs(across - down) < HALF // 4
    return jnp.where(near, jnp.concatenate([value, value], axis=0), 0.0)


def unpack(packed, lead_ref, trail_ref):
    across, down = grid_of(HALF)
    ahead = across - down
    even = (ahead[:SPAN] & 1) == 0
    shared = packed[SPAN : 2 * SPAN]
    square = jnp.concatenate(
        [
            packed[:SPAN],
            jnp.where(even, shared, 0.0),
            pltpu.roll(jnp.where(even, 0.0, shared), HALF - 1, 1),
            packed[2 * SPAN :],
        ],
        axis=0,
    )

    def symmetric(moved):
        upper = pltpu.roll(square, HALF - moved, 1)
        upper = jnp.where(jnp.logical_and(ahead >= 0, ahead < REACH), upper, 0.0)
        return fold(jnp.where(ahead >= 0, upper, upper.T))

    cross = jnp.where(jnp.abs(ahead) < REACH, square, 0.0)
    lead_ref[: HALF // 2] = symmetric(SPAN)
    lead_ref[HALF // 2 :] = fold(cross.T)
    trail_ref[: HALF // 2] = fold(cross)
    trail_ref[HALF // 2 :] = symmetric(2 * SPAN)


def add_gram(total_ref, panel):
    high, low = split(panel)
    total_ref[...] += dot_rows(high, jnp.concatenate([high, low], axis=1))


def first_gram_kernel(panel_hbm, square_ref, panel_ref, total_ref, sems):
    copies = []
    for number in range(panel_hbm.shape[0] // GRAM_CHUNK):
        rows = pl.ds(number * GRAM_CHUNK, GRAM_CHUNK)
        copy = pltpu.make_async_copy(panel_hbm.at[rows], panel_ref.at[rows], sems.at[number])
        copy.start()
        copies.append((rows, copy))
    total_ref[...] = jnp.zeros_like(total_ref)
    for rows, copy in copies:
        copy.wait()
        add_gram(total_ref, panel_ref[rows])
    pack(total_ref, None, square_ref)


def is_odd():
    return lax.axis_index("pair") % 2 == 1


def second_gram_kernel(is_first, is_last, *refs):
    before_ref = None
    if not is_first:
        before_ref, *refs = refs
    far_ref, near_ref, *refs = refs
    if is_last:
        square_ref, *refs = refs
    (total_ref,) = refs
    if is_first:
        total_ref[...] = jnp.zeros_like(total_ref)
    else:
        total_ref[...] = before_ref[...]
    for number in range(near_ref.shape[0] // CHUNK):
        rows = pl.ds(number * CHUNK, CHUNK)
        add_gram(total_ref, jnp.concatenate([far_ref[rows], near_ref[rows]], axis=1))
    if is_last:
        pack(total_ref, is_odd(), square_ref)


VMEM = pltpu.VMEM
SQUARE = VMEM((3 * SPAN, HALF), f32)
TOTAL = VMEM((2 * HALF, 4 * HALF), f32)
IN_VMEM = pl.BlockSpec(memory_space=pltpu.VMEM)
IN_HBM = pl.BlockSpec(memory_space=pltpu.HBM)
DMA = pltpu.SemaphoreType.DMA


def in_vmem(*values):
    return [pltpu.with_memory_space_constraint(value, pltpu.VMEM) for value in values]


def in_hbm(value):
    return pltpu.with_memory_space_constraint(value, pltpu.HBM)


def params():
    return pltpu.CompilerParams(vmem_limit_bytes=16 * 2**20)


def cost(rows):
    return pl.CostEstimate(
        flops=2 * 3 * rows * 4 * HALF * HALF, bytes_accessed=16 * rows * HALF, transcendentals=0
    )


def first_gram(panel):
    rows = panel.shape[0]
    return pl.pallas_call(
        first_gram_kernel,
        out_shape=(SQUARE, VMEM(panel.shape, f32)),
        in_specs=[IN_HBM],
        out_specs=(IN_VMEM, IN_VMEM),
        scratch_shapes=[TOTAL, DMA((rows // GRAM_CHUNK,))],
        compiler_params=params(),
        cost_estimate=cost(rows),
    )(in_hbm(panel))


def second_gram(before, is_last, far, near):
    befores = [] if before is None else [before]
    operands = in_vmem(*befores, far, near)
    return pl.pallas_call(
        functools.partial(second_gram_kernel, before is None, is_last),
        out_shape=SQUARE if is_last else TOTAL,
        in_specs=[IN_VMEM] * len(operands),
        out_specs=IN_VMEM,
        scratch_shapes=[TOTAL] if is_last else [],
        compiler_params=params(),
        cost_estimate=cost(near.shape[0]),
    )(*operands)


def rotate(leading, trailing, cos_row, sin_row):
    return cos_row * leading - sin_row * trailing, sin_row * leading + cos_row * trailing


def move(first, second, across):
    moved = pltpu.roll(jnp.where(across == 0, second, first), 1, 1)
    top = jnp.where(across == 0, first, moved)
    bottom = jnp.where(across == HALF - 1, first, pltpu.roll(second, HALF - 1, 1))
    return top, bottom


def half_angle(first, coupling, second):
    along = first - second
    up = -2.0 * coupling
    along_size = jnp.abs(along)
    up_size = jnp.abs(up)
    scale = jnp.maximum(along_size, up_size)
    flat = scale == 0.0
    inverse = pl.reciprocal(jnp.where(flat, 1.0, scale), approx=True)
    along_part = jnp.where(flat, 1.0, along_size * inverse)
    up_part = up_size * inverse
    length = lax.rsqrt(along_part * along_part + up_part * up_part)
    square = 0.5 + 0.5 * (along_part * length)
    root = lax.rsqrt(square)
    large = square * root
    small = 0.5 * (up_part * length) * root
    ahead = along >= 0.0
    cos_part = jnp.where(ahead, large, small)
    sin_part = jnp.where(ahead, small, large)
    return cos_part, jnp.where(up > 0.0, sin_part, -sin_part)


def eigensolve(lead_ref, trail_ref, basis_lead_ref, basis_trail_ref):
    across, down = grid_of(HALF)
    half = HALF // 2
    mask = jnp.logical_and((across & (half - 1)) == (down & (half - 1)), down < half)
    basis_lead_ref[...] = jnp.where(mask, 1.0, 0.0)
    basis_trail_ref[...] = jnp.where(
        jnp.logical_and((across & (half - 1)) == (down & (half - 1)), down >= half), 1.0, 0.0
    )

    def column_sums(value):
        return jnp.sum(value, axis=0, keepdims=True)

    def step(number, carried):
        turns = half_angle(*carried)
        product = rotate(lead_ref[...], trail_ref[...], *turns)
        basis = rotate(basis_lead_ref[...], basis_trail_ref[...], *turns)
        first, second = move(
            column_sums(product[0] * basis[0]), column_sums(product[1] * basis[1]), across[:1]
        )
        lead_ref[...], trail = move(*product, across)
        trail_ref[...] = trail
        basis_lead, basis_trail_ref[...] = move(*basis, across)
        basis_lead_ref[...] = basis_lead
        return first, column_sums(basis_lead * trail), second

    def diagonal_of(folded):
        return column_sums(jnp.where(mask[:half], folded, 0.0))

    first, _, second = lax.fori_loop(
        0,
        STEPS,
        step,
        (diagonal_of(lead_ref[:half]), diagonal_of(trail_ref[:half]), diagonal_of(trail_ref[half:])),
        unroll=4,
    )
    return jnp.concatenate([first, second], axis=1)


def restored_basis(basis_lead_ref, basis_trail_ref, table):
    half = HALF // 2
    basis = jnp.concatenate(
        [
            jnp.concatenate([unfold(ref[:half]), unfold(ref[half:])], axis=0)
            for ref in (basis_lead_ref, basis_trail_ref)
        ],
        axis=1,
    )
    high, low = split(basis)
    return dot(high, table).astype(bf16), dot(low, table).astype(bf16)


def product(panel, basis_high, basis_low):
    high, low = split(panel)
    return dot(high, basis_high) + (dot(high, basis_low) + dot(low, basis_high))


def project(panel_ref, basis, start, near_ref, far_ref):
    for number in range(near_ref.shape[0] // CHUNK):
        rows = pl.ds(number * CHUNK, CHUNK)
        value = product(panel_ref[pl.ds(start + number * CHUNK, CHUNK)], *basis)
        near_ref[rows] = value[:, :HALF]
        far_ref[rows] = value[:, HALF:]


def first_round_kernel(
    *refs,
):
    *parts, table_ref, panel_ref, near_ref, far_ref, high_ref, low_ref = refs[:10]
    scratch = refs[10:]
    unpack(total_of(parts), *scratch[:2])
    eigensolve(*scratch)
    swapped = jnp.logical_or(lax.axis_index("pair") == 0, is_odd())
    basis = [
        jnp.where(swapped, jnp.concatenate([value[:, HALF:], value[:, :HALF]], axis=1), value)
        for value in restored_basis(*scratch[2:], table_ref[...])
    ]
    project(panel_ref, basis, 0, near_ref, far_ref)
    high_ref[...], low_ref[...] = basis


def later_rows_kernel(high_ref, low_ref, panel_ref, *outs):
    start = CHUNKS[0]
    for part in range(0, len(outs), 2):
        project(panel_ref, (high_ref[...], low_ref[...]), start, *outs[part : part + 2])
        start += outs[part].shape[0]


def solve_scratch():
    return [VMEM((HALF, HALF), f32)] * 4


def first_round(sums, table, panel):
    basis = VMEM((2 * HALF, 2 * HALF), bf16)
    near, far, high, low = pl.pallas_call(
        first_round_kernel,
        out_shape=[VMEM((CHUNKS[0], HALF), f32)] * 2 + [basis] * 2,
        in_specs=[IN_VMEM] * 6,
        out_specs=[IN_VMEM] * 4,
        scratch_shapes=solve_scratch(),
        compiler_params=params(),
    )(*in_vmem(*sums, table, panel))
    later = pl.pallas_call(
        later_rows_kernel,
        out_shape=[VMEM((chunk, HALF), f32) for chunk in CHUNKS[1:] for _ in range(2)],
        in_specs=[IN_VMEM] * 3,
        out_specs=[IN_VMEM] * (2 * len(CHUNKS) - 2),
        compiler_params=params(),
        cost_estimate=cost(sum(CHUNKS[1:])),
    )(*in_vmem(high, low, panel))
    return [near, far] + list(later)


def second_round_kernel(parts, *refs):
    parts_of_sum, (table_ref, *refs) = refs[:4], refs[4:]
    sources, refs = refs[: 2 * parts], refs[2 * parts :]
    magnitudes_hbm, energies_ref, out_ref, *scratch, sems = refs
    unpack(total_of(parts_of_sum), *scratch[:2])
    squares = eigensolve(*scratch)
    table = table_ref[...]
    basis = [
        jnp.where(is_odd(), jnp.concatenate([value[HALF:], value[:HALF]], axis=0), value)
        for value in restored_basis(*scratch[2:], table)
    ]
    copies = []
    for part in range(parts):
        far_ref, near_ref = sources[2 * part : 2 * part + 2]
        for number in range(near_ref.shape[0] // CHUNK):
            rows = pl.ds(len(copies) * CHUNK, CHUNK)
            source = pl.ds(number * CHUNK, CHUNK)
            panel = jnp.concatenate([far_ref[source], near_ref[source]], axis=1)
            out_ref[rows] = jnp.abs(product(panel, *basis))
            copy = pltpu.make_async_copy(
                out_ref.at[rows], magnitudes_hbm.at[rows], sems.at[len(copies)]
            )
            copy.start()
            copies.append(copy)
    squares = jnp.dot(
        jnp.broadcast_to(squares, (8, 2 * HALF)),
        table.astype(f32),
        precision=lax.Precision.HIGHEST,
        preferred_element_type=f32,
    )
    total_rows = lax.axis_size("row") * out_ref.shape[0]
    energies_ref[...] = squares[:1] * (1.0 / total_rows)
    for copy in copies:
        copy.wait()


def second_round(sums, table, parts):
    rows = sum(part[0].shape[0] for part in parts)
    shape = (rows, 2 * HALF)
    operands = in_vmem(*sums, table, *[value for part in parts for value in part])
    return pl.pallas_call(
        functools.partial(second_round_kernel, len(parts)),
        out_shape=(pltpu.HBM(shape, f32), jax.ShapeDtypeStruct((1, 2 * HALF), f32)),
        in_specs=[IN_VMEM] * len(operands),
        out_specs=(IN_HBM, IN_VMEM),
        scratch_shapes=[VMEM(shape, f32)] + solve_scratch() + [DMA((rows // CHUNK,))],
        compiler_params=params(),
    )(*operands)


def row_sum(square):
    count = lax.axis_size("row")

    def shifted(value, chips):
        return lax.ppermute(value, "row", [(at, (at + 2 * chips) % count) for at in range(count)])

    square = square + lax.ppermute(square, "row", [(at, at ^ 1) for at in range(count)])
    return shifted(square, -1), shifted(square, 1), square, shifted(square, 2)


def total_of(parts):
    behind, ahead, own, across = [part[...] for part in parts]
    return (behind + ahead) + (own + across)


def exchange(near, far):
    last = lax.axis_size("pair") - 1
    inner = [(at, at - 1 + 2 * (at % 2)) for at in range(1, last)]
    return (
        lax.ppermute(far, "pair", [(0, 0)] + inner + [(last, last)]),
        lax.ppermute(near, "pair", [(at, at ^ 1) for at in range(last + 1)]),
    )


def body(matrix):
    table = jnp.asarray(restore_table(2 * HALF, STEPS), dtype=bf16)
    square, panel = first_gram(matrix)
    blocks = first_round(row_sum(square), table, panel)
    parts = [exchange(*blocks[at : at + 2]) for at in range(0, len(blocks), 2)]
    total = None
    for number, part in enumerate(parts):
        total = second_gram(total, number == len(parts) - 1, *part)
    magnitudes, energies = second_round(row_sum(total), table, parts)
    return magnitudes, energies.reshape(2 * HALF)


def solution(mesh):
    return jax.shard_map(
        body,
        mesh=mesh,
        in_specs=(P("row", "pair"),),
        out_specs=(P("row", "pair"), P("pair")),
        check_vma=False,
    )
```
